32 devices in a mesh: dp: 8 (over y, x, core), fsdp: 4 (over z).
Axes of the slice: x: 2, y: 2, z: 4, core: 2. Of those that a mesh axis runs over, the one named last changes fastest.
Arguments:
- tokens: bfloat16 [16384, 1024], P(('dp', 'fsdp')), may hold values from -6 to 6
- segments: int32 [16384], P(('dp', 'fsdp')), may hold values from -1 to 1, as said below
- qkv_weight: bfloat16 [1024, 3072], P('fsdp'), may hold values from -6 to 6
- out_weight: bfloat16 [1024, 1024], P('fsdp'), may hold values from -0.1875 to 0.1875
Outputs:
- projected: bfloat16 [16384, 1024], P(('dp', 'fsdp'))
The draws below stay inside these ranges and needn't reach their ends.
Inputs may be any that keep to these rules, and one draw needn't show every extreme that they name: `segments`: each image lies inside one block of 256 rows and is numbered 0 or 1 there; -1 marks empty rows. Each device's 512 rows begin with 0 to 2 blocks that hold images, its other blocks are empty. Two devices with equal fsdp index whose dp indices differ by half the dp axis hold 2 such blocks together; the first device holds 2.
All inputs are finite; a program needn't handle non-finite values.
Results may differ from the reference program's by a relative error of at most 0.0089.
Values may be sent and summed in bfloat16 or wider, within the bound.
A program may use at most 64 MiB of HBM per device.

```python
import jax
import jax.numpy as jnp
from jax import lax

D = 1024
HEADS = 16
BLK = 256
NB = 2
ROWS_DEV = 512
ROWS = 16384


def draw_segments(key, part):
    device_count = ROWS // ROWS_DEV
    half_count = device_count // 2
    key_count, key_first, key_pad = jax.random.split(key, 3)
    first_half = jax.random.randint(key_count, (half_count,), 0, NB + 1)
    first_half = first_half.at[0].set(NB)
    live_count = jnp.concatenate([first_half, NB - first_half])
    first_len = jax.random.randint(key_first, (device_count, NB), BLK // 4, BLK // 2 + 1)
    padding = jax.random.randint(key_pad, (device_count, NB), 0, BLK // 4)
    second_end = BLK - padding
    position = jnp.arange(BLK)[None, None, :]
    image_ids = jnp.where(position < first_len[..., None], 0, jnp.where(position < second_end[..., None], 1, -1))
    live_block = jnp.arange(NB)[None, :] < live_count[:, None]
    image_ids = jnp.where(live_block[..., None], image_ids, -1)
    return image_ids.reshape(ROWS).astype(jnp.int32)


def draw_qkv_weight(key, part):
    spread = D ** (-0.5)
    return (jax.random.normal(key, (D, 3 * D), jnp.float32) * spread).astype(jnp.bfloat16)


def block_levels(stream_key, dims, cuts, least, top_value):
    factor_of, own = 1.0, jax.random.fold_in(stream_key, 6)
    for dim, parts in cuts:
        draws = jnp.exp(jax.random.uniform(jax.random.fold_in(own, dim), (parts,), jnp.float32, least / len(cuts), top_value / len(cuts)))
        factor_of = factor_of * jnp.repeat(draws, dims[dim] // parts).reshape([-1 if axis == dim else 1 for axis in range(len(dims))])
    return factor_of


def normal_values(rng, shape, scale, bound, shards=(), held_as=jnp.bfloat16):
    values = scale * jax.random.normal(rng, shape, jnp.float32)
    if shards:
        values = values * block_levels(rng, shape, shards, -0.22, 0.18)
    return jnp.clip(values, -bound, bound).astype(held_as)


def setup_inputs(seed: int = 0) -> dict:
    key_of = jax.random.split(jax.random.key(seed), 5)
    return {
        "tokens": normal_values(key_of[0], (ROWS, D), 1.0, 6.0, ((0, 32),)),
        "segments": draw_segments(jax.random.fold_in(key_of[4], 71), 0),
        "qkv_weight": draw_qkv_weight(jax.random.fold_in(key_of[4], 71), 0),
        "out_weight": normal_values(key_of[3], (D, D), D ** -0.5, 0.1875, ((0, 4),)),
    }


def normalize(block_rows):
    values_f = block_rows.astype(jnp.float32)
    row_mean = lax.optimization_barrier(jnp.mean(values_f, axis=-1, keepdims=True))
    centered = values_f - row_mean
    variance = lax.optimization_barrier(jnp.mean(centered * centered, axis=-1, keepdims=True))
    return (centered * lax.rsqrt(variance + 1e-05)).astype(jnp.bfloat16)

def attend(packed_qkv, segment, head_count):
    row_count = packed_qkv.shape[0]
    model_width = packed_qkv.shape[1] // 3
    head_dim = model_width // head_count
    queries = packed_qkv[:, :model_width].reshape(row_count, head_count, head_dim).astype(jnp.float32)
    key_rows = packed_qkv[:, model_width:2 * model_width].reshape(row_count, head_count, head_dim).astype(jnp.float32)
    values = packed_qkv[:, 2 * model_width:].reshape(row_count, head_count, head_dim).astype(jnp.float32)
    scores = jnp.einsum('qhd,khd->hqk', queries, key_rows) * head_dim ** (-0.5)
    same_image = segment[:, None] == segment[None, :]
    scores = jnp.where(same_image[None], scores, -1e+30)
    row_max = lax.optimization_barrier(jnp.max(scores, axis=-1, keepdims=True))
    weights = jnp.exp(scores - row_max)
    row_total = lax.optimization_barrier(jnp.sum(weights, axis=-1, keepdims=True))
    attention = (weights / row_total).astype(jnp.bfloat16)
    mixed_rows = jnp.einsum('hqk,khd->qhd', attention.astype(jnp.float32), values)
    return mixed_rows.reshape(row_count, model_width).astype(jnp.bfloat16)

def sublayer(token_rows, segment, qkv_weight, out_weight):
    normed = normalize(token_rows)
    packed_qkv = jnp.dot(normed, qkv_weight, preferred_element_type=jnp.float32).astype(jnp.bfloat16)
    mixed_rows = attend(packed_qkv, segment, HEADS)
    result = jnp.dot(mixed_rows, out_weight, preferred_element_type=jnp.float32)
    return jnp.where(segment[:, None] >= 0, result, 0.0).astype(jnp.bfloat16)

def reference(tokens, segments, qkv_weight, out_weight):
    block_count = ROWS // BLK
    block_tokens = tokens.reshape(block_count, BLK, D)
    block_segments = segments.reshape(block_count, BLK)

    def one_block(operands):
        return sublayer(operands[0], operands[1], qkv_weight, out_weight)
    out_blocks = lax.map(one_block, (block_tokens, block_segments))
    return out_blocks.reshape(ROWS, D)
```

```python
import functools
import math

import jax
import jax.numpy as jnp
from jax import lax
from jax.experimental import pallas as pl
from jax.experimental.pallas import tpu as pltpu
from jax.sharding import PartitionSpec as P

HEADS = 16
BLK = 256
LOG2E = math.log2(math.e)
MESH = pl.DeviceIdType.MESH


def rows_of(start, count):
    return pl.ds(pl.multiple_of(start, count), count)


def kernel(
    shards,
    tok_ref,
    seg_ref,
    qkv_ref,
    ow_ref,
    out_ref,
    wbuf,
    obuf,
    nbuf,
    segbuf,
    bias,
    sendbuf,
    mix,
    local_sem,
    z_send,
    z_recv,
    x_send,
    x_recv,
    y_send,
    y_recv,
    d_send,
    d_recv,
    o_send,
    o_recv,
    m_send,
    m_recv,
    t_send,
    t_recv,
):
    rows, width = tok_ref.shape
    head_dim = width // HEADS
    pair = 2 * head_dim
    half = width // 2
    groups = half // pair
    shard = qkv_ref.shape[0]
    quarter = shard // 4
    blocks = rows // BLK
    steps = range(1, shards)

    dp = lax.axis_index("dp")
    z = lax.axis_index("fsdp")
    core = lax.rem(dp, 2)
    x = lax.rem(dp // 2, 2)
    y = lax.rem(dp // 4, 2)
    x_dev = (dp + 2 - 4 * x, z)
    y_dev = (dp + 4 - 8 * y, z)
    c_dev = (dp + 1 - 2 * core, z)
    other = 1 - core
    part = 2 * y + x
    x_part = 2 * y + 1 - x
    y_part = 2 * (1 - y) + x
    d_part = 2 * (1 - y) + 1 - x

    def ahead(s):
        return lax.rem(z + s, shards)

    def behind(s):
        return lax.rem(z + shards - s, shards)

    def place(k, source, piece):
        where = rows_of(source * shard + piece * quarter, quarter)
        if k < groups:
            return wbuf.at[k, where, :]
        return obuf.at[core, where, :]

    def remote(ref, send, recv, device):
        return pltpu.make_async_remote_copy(
            src_ref=ref, dst_ref=ref, send_sem=send, recv_sem=recv, device_id=device, device_id_type=MESH
        )

    own = rows_of(z * shard, shard)
    local = []
    for k in range(groups):
        local.append(
            [
                pltpu.make_async_copy(
                    qkv_ref.at[:, pl.ds(pl.multiple_of(j * width + core * half + k * pair, pair), pair)],
                    wbuf.at[k, own, j * pair : (j + 1) * pair],
                    local_sem.at[3 * k + j],
                )
                for j in range(3)
            ]
        )
    local.append(
        [
            pltpu.make_async_copy(
                ow_ref.at[:, h * half : (h + 1) * half], obuf.at[h, own, :], local_sem.at[3 * groups + h]
            )
            for h in range(2)
        ]
    )
    for copies in local:
        for copy in copies:
            copy.start()

    barrier = pltpu.get_barrier_semaphore()
    for s in steps:
        pl.semaphore_signal(barrier, inc=1, device_id=(dp, ahead(s)), device_id_type=MESH)
    for device in (x_dev, y_dev, c_dev):
        pl.semaphore_signal(barrier, inc=1, device_id=device, device_id_type=MESH)
    pl.semaphore_wait(barrier, shards + 2)

    pending = []

    def start(copy):
        copy.start()
        pending.append(copy)

    def z_copy(k, s, source, device):
        return remote(place(k, source, part), z_send.at[k, s - 1], z_recv.at[k, s - 1], device)

    for k in range(groups + 1):
        for copy in local[k]:
            copy.wait()
        for s in steps:
            start(z_copy(k, s, z, (dp, ahead(s))))

    segbuf[core] = jnp.broadcast_to(seg_ref[...], segbuf.shape[1:])
    seg_copy = remote(segbuf.at[core], t_send.at[0], t_recv.at[0], c_dev)
    start(seg_copy)

    tile = 64

    @pl.loop(0, rows // tile)
    def _(i):
        where = rows_of(i * tile, tile)
        values = tok_ref[where, :].astype(jnp.float32)
        centered = values - jnp.mean(values, axis=-1, keepdims=True)
        variance = jnp.mean(centered * centered, axis=-1, keepdims=True)
        nbuf[core, where, :] = (centered * lax.rsqrt(variance + 1e-05)).astype(jnp.bfloat16)

    start(remote(nbuf.at[core], t_send.at[1], t_recv.at[1], c_dev))
    remote(segbuf.at[other], t_send.at[0], t_recv.at[0], c_dev).wait_recv()

    for c in range(2):
        for b in range(blocks):
            ids = segbuf[c, 0:1, b * BLK : (b + 1) * BLK].astype(jnp.float32)
            along = jnp.broadcast_to(ids, (BLK, BLK))
            bias[c, b] = jnp.where(along == along.T, 0.0, -1e30)

    def x_copy(k, s, piece):
        return remote(place(k, behind(s), piece), x_send.at[k, s - 1], x_recv.at[k, s - 1], x_dev)

    def y_copy(k, s, piece):
        return remote(place(k, behind(s), piece), y_send.at[k, s - 1], y_recv.at[k, s - 1], y_dev)

    def d_copy(k, s, piece, device):
        return remote(place(k, behind(s), piece), d_send.at[k, s - 1], d_recv.at[k, s - 1], device)

    def by_x(k, s):
        return (k + s) % 2 == 0

    def spread(k):
        for s in steps:
            z_copy(k, s, behind(s), (dp, ahead(s))).wait_recv()
            start(x_copy(k, s, part))
            start(y_copy(k, s, part))

    def cross(k):
        for s in steps:
            if by_x(k, s):
                x_copy(k, s, x_part).wait_recv()
                start(d_copy(k, s, x_part, y_dev))
            else:
                y_copy(k, s, y_part).wait_recv()
                start(d_copy(k, s, y_part, x_dev))

    def finish(k, s):
        if by_x(k, s):
            y_copy(k, s, y_part).wait_recv()
            d_copy(k, s, d_part, y_dev).wait_recv()
        else:
            x_copy(k, s, x_part).wait_recv()
            d_copy(k, s, d_part, x_dev).wait_recv()

    lane = lax.broadcasted_iota(jnp.int32, (BLK, pair), 1)
    first = lane < head_dim

    def attend(k, owner, b):
        where = rows_of(b * BLK, BLK)
        packed = jnp.dot(
            nbuf[owner, where, :], wbuf[k], preferred_element_type=jnp.float32
        ).astype(jnp.bfloat16)
        queries = packed[:, :pair]
        keys = packed[:, pair : 2 * pair]
        values = packed[:, 2 * pair :]
        zero = jnp.zeros_like(queries)
        one = jnp.ones_like(values)
        mixed = []
        for keep in (first, ~first):
            scores = lax.dot_general(
                jnp.where(keep, queries, zero), keys, (((1,), (1,)), ((), ())), preferred_element_type=jnp.float32
            )
            scores = scores * (LOG2E * head_dim ** (-0.5)) + bias[owner, b]
            weights = jnp.exp2(scores - jnp.max(scores, axis=-1, keepdims=True)).astype(jnp.bfloat16)
            mixed.append(
                jnp.dot(weights, jnp.where(keep, values, one), preferred_element_type=jnp.float32)
            )
        totals = pltpu.roll(jnp.where(first, mixed[1], mixed[0]), head_dim, 1)
        return (jnp.where(first, mixed[0], mixed[1]) / totals).astype(jnp.bfloat16)

    def m_copy(k, owner):
        return pltpu.make_async_remote_copy(
            src_ref=sendbuf.at[k],
            dst_ref=mix.at[owner * groups + k],
            send_sem=m_send.at[k],
            recv_sem=m_recv.at[k],
            device_id=c_dev,
            device_id_type=MESH,
        )

    def theirs(k):
        for s in steps:
            finish(k, s)

        @pl.loop(0, blocks)
        def _(b):
            sendbuf[k, rows_of(b * BLK, BLK), :] = attend(k, other, b)

        start(m_copy(k, core))

    def mine(k):
        @pl.loop(0, blocks)
        def _(b):
            mix[core * groups + k, rows_of(b * BLK, BLK), :] = attend(k, core, b)

    spread(0)
    spread(1)
    cross(0)
    spread(2)
    cross(1)
    remote(nbuf.at[other], t_send.at[1], t_recv.at[1], c_dev).wait_recv()
    for k in range(groups):
        theirs(k)
        if k + 3 <= groups:
            spread(k + 3)
        if k + 2 <= groups:
            cross(k + 2)
        mine(k)

    def o_copy(s, owner):
        where = rows_of(behind(s) * shard, shard)
        return remote(obuf.at[owner, where, :], o_send.at[s - 1], o_recv.at[s - 1], c_dev)

    for s in steps:
        finish(groups, s)
        start(o_copy(s, core))
    for k in range(groups):
        m_copy(k, other).wait_recv()

    def project(h):
        @pl.loop(0, blocks)
        def _(b):
            where = rows_of(b * BLK, BLK)
            mixed = jnp.concatenate([mix[j, where, :] for j in range(2 * groups)], axis=1)
            result = jnp.dot(mixed, obuf[h], preferred_element_type=jnp.float32)
            ids = jnp.broadcast_to(segbuf[core, 0:1, where].astype(jnp.float32), (pair, BLK)).T
            keep = jnp.concatenate([ids] * (half // pair), axis=1) >= 0.0
            out_ref[where, pl.ds(pl.multiple_of(h * half, half), half)] = jnp.where(keep, result, 0.0).astype(
                jnp.bfloat16
            )

    project(core)
    for s in steps:
        o_copy(s, other).wait_recv()
    project(other)
    for copy in pending:
        copy.wait_send()


def body(tokens, segments, qkv_weight, out_weight, shards):
    rows, width = tokens.shape
    half = width // 2
    pair = 2 * (width // HEADS)
    groups = half // pair
    blocks = rows // BLK
    vmem = pl.BlockSpec(memory_space=pltpu.VMEM)
    hbm = pl.BlockSpec(memory_space=pl.ANY)
    bf16 = jnp.bfloat16
    dma = pltpu.SemaphoreType.DMA
    sets = dma((groups + 1, shards - 1))
    return pl.pallas_call(
        functools.partial(kernel, shards),
        out_shape=jax.ShapeDtypeStruct((rows, width), bf16),
        in_specs=[vmem, vmem, hbm, hbm],
        out_specs=vmem,
        scratch_shapes=[
            pltpu.VMEM((groups, width, 3 * pair), bf16),
            pltpu.VMEM((2, width, half), bf16),
            pltpu.VMEM((2, rows, width), bf16),
            pltpu.VMEM((2, 8, rows), jnp.int32),
            pltpu.VMEM((2, blocks, BLK, BLK), jnp.float32),
            pltpu.VMEM((groups, rows, pair), bf16),
            pltpu.VMEM((2 * groups, rows, pair), bf16),
            dma((3 * groups + 2,)),
            *([sets] * 8),
            dma((shards - 1,)),
            dma((shards - 1,)),
            dma((groups,)),
            dma((groups,)),
            dma((2,)),
            dma((2,)),
        ],
        compiler_params=pltpu.CompilerParams(
            collective_id=0, has_side_effects=True, vmem_limit_bytes=48 * 1024 * 1024
        ),
    )(tokens, segments.reshape(1, rows), qkv_weight, out_weight)


def solution(mesh):
    return jax.shard_map(
        functools.partial(body, shards=mesh.shape["fsdp"]),
        mesh=mesh,
        in_specs=(P(("dp", "fsdp"), None), P(("dp", "fsdp")), P("fsdp", None), P("fsdp", None)),
        out_specs=P(("dp", "fsdp"), None),
        check_vma=False,
    )
```

```python
import functools
import math

import jax
import jax.numpy as jnp
from jax import lax
from jax.experimental import pallas as pl
from jax.experimental.pallas import tpu as pltpu
from jax.sharding import PartitionSpec as P

HEADS = 16
BLK = 256
LOG2E = math.log2(math.e)
MESH = pl.DeviceIdType.MESH


def rows_of(start, count):
    return pl.ds(pl.multiple_of(start, count), count)


def kernel(
    shards,
    tok_ref,
    seg_ref,
    qkv_ref,
    ow_ref,
    out_ref,
    wbuf,
    obuf,
    nbuf,
    segbuf,
    bias,
    sendbuf,
    mix,
    local_sem,
    z_send,
    z_recv,
    x_send,
    x_recv,
    y_send,
    y_recv,
    d_send,
    d_recv,
    o_send,
    o_recv,
    m_send,
    m_recv,
    t_send,
    t_recv,
):
    rows, width = tok_ref.shape
    head_dim = width // HEADS
    pair = 2 * head_dim
    half = width // 2
    groups = half // pair
    shard = qkv_ref.shape[0]
    quarter = shard // 4
    blocks = rows // BLK
    steps = range(1, shards)

    dp = lax.axis_index("dp")
    z = lax.axis_index("fsdp")
    core = lax.rem(dp, 2)
    x = lax.rem(dp // 2, 2)
    y = lax.rem(dp // 4, 2)
    x_dev = (dp + 2 - 4 * x, z)
    y_dev = (dp + 4 - 8 * y, z)
    c_dev = (dp + 1 - 2 * core, z)
    other = 1 - core
    part = 2 * y + x
    x_part = 2 * y + 1 - x
    y_part = 2 * (1 - y) + x
    d_part = 2 * (1 - y) + 1 - x

    def ahead(s):
        return lax.rem(z + s, shards)

    def behind(s):
        return lax.rem(z + shards - s, shards)

    def place(k, source, piece):
        where = rows_of(source * shard + piece * quarter, quarter)
        if k < groups:
            return wbuf.at[k, where, :]
        return obuf.at[core, where, :]

    def remote(ref, send, recv, device):
        return pltpu.make_async_remote_copy(
            src_ref=ref, dst_ref=ref, send_sem=send, recv_sem=recv, device_id=device, device_id_type=MESH
        )

    own = rows_of(z * shard, shard)
    local = []
    for k in range(groups):
        local.append(
            [
                pltpu.make_async_copy(
                    qkv_ref.at[:, pl.ds(pl.multiple_of(j * width + core * half + k * pair, pair), pair)],
                    wbuf.at[k, own, j * pair : (j + 1) * pair],
                    local_sem.at[3 * k + j],
                )
                for j in range(3)
            ]
        )
    local.append(
        [
            pltpu.make_async_copy(
                ow_ref.at[:, h * half : (h + 1) * half], obuf.at[h, own, :], local_sem.at[3 * groups + h]
            )
            for h in range(2)
        ]
    )
    for copies in local:
        for copy in copies:
            copy.start()

    barrier = pltpu.get_barrier_semaphore()
    for s in steps:
        pl.semaphore_signal(barrier, inc=1, device_id=(dp, ahead(s)), device_id_type=MESH)
    for device in (x_dev, y_dev, c_dev):
        pl.semaphore_signal(barrier, inc=1, device_id=device, device_id_type=MESH)
    pl.semaphore_wait(barrier, shards + 2)

    pending = []

    def start(copy):
        copy.start()
        pending.append(copy)

    def z_copy(k, s, source, device):
        return remote(place(k, source, part), z_send.at[k, s - 1], z_recv.at[k, s - 1], device)

    def launch(k):
        if k <= groups:
            for copy in local[k]:
                copy.wait()
            for s in steps:
                start(z_copy(k, s, z, (dp, ahead(s))))

    launch(0)
    launch(1)

    segbuf[core] = jnp.broadcast_to(seg_ref[...], segbuf.shape[1:])
    seg_copy = remote(segbuf.at[core], t_send.at[0], t_recv.at[0], c_dev)
    start(seg_copy)

    tile = 64

    @pl.loop(0, rows // tile)
    def _(i):
        where = rows_of(i * tile, tile)
        values = tok_ref[where, :].astype(jnp.float32)
        centered = values - jnp.mean(values, axis=-1, keepdims=True)
        variance = jnp.mean(centered * centered, axis=-1, keepdims=True)
        nbuf[core, where, :] = (centered * lax.rsqrt(variance + 1e-05)).astype(jnp.bfloat16)

    start(remote(nbuf.at[core], t_send.at[1], t_recv.at[1], c_dev))
    remote(segbuf.at[other], t_send.at[0], t_recv.at[0], c_dev).wait_recv()

    for c in range(2):
        for b in range(blocks):
            ids = segbuf[c, 0:1, b * BLK : (b + 1) * BLK].astype(jnp.float32)
            along = jnp.broadcast_to(ids, (BLK, BLK))
            bias[c, b] = jnp.where(along == along.T, 0.0, -1e30)

    def x_copy(k, s, piece):
        return remote(place(k, behind(s), piece), x_send.at[k, s - 1], x_recv.at[k, s - 1], x_dev)

    def y_copy(k, s, piece):
        return remote(place(k, behind(s), piece), y_send.at[k, s - 1], y_recv.at[k, s - 1], y_dev)

    def d_copy(k, s, piece, device):
        return remote(place(k, behind(s), piece), d_send.at[k, s - 1], d_recv.at[k, s - 1], device)

    def by_x(k, s):
        return (k + s) % 2 == 0

    def spread_one(k, s):
        z_copy(k, s, behind(s), (dp, ahead(s))).wait_recv()
        start(x_copy(k, s, part))
        start(y_copy(k, s, part))

    def cross_one(k, s):
        if by_x(k, s):
            x_copy(k, s, x_part).wait_recv()
            start(d_copy(k, s, x_part, y_dev))
        else:
            y_copy(k, s, y_part).wait_recv()
            start(d_copy(k, s, y_part, x_dev))

    def spread(k):
        launch(k + 2)
        for s in steps:
            spread_one(k, s)

    def cross(k):
        for s in steps:
            cross_one(k, s)

    def finish(k, s):
        if by_x(k, s):
            y_copy(k, s, y_part).wait_recv()
            d_copy(k, s, d_part, y_dev).wait_recv()
        else:
            x_copy(k, s, x_part).wait_recv()
            d_copy(k, s, d_part, x_dev).wait_recv()

    lane = lax.broadcasted_iota(jnp.int32, (BLK, pair), 1)
    first = lane < head_dim

    def attend(k, owner, b):
        where = rows_of(b * BLK, BLK)
        packed = jnp.dot(
            nbuf[owner, where, :], wbuf[k], preferred_element_type=jnp.float32
        ).astype(jnp.bfloat16)
        queries = packed[:, :pair]
        keys = packed[:, pair : 2 * pair]
        values = packed[:, 2 * pair :]
        zero = jnp.zeros_like(queries)
        one = jnp.ones_like(values)
        mixed = []
        for keep in (first, ~first):
            scores = lax.dot_general(
                jnp.where(keep, queries, zero), keys, (((1,), (1,)), ((), ())), preferred_element_type=jnp.float32
            )
            scores = scores * (LOG2E * head_dim ** (-0.5)) + bias[owner, b]
            weights = jnp.exp2(scores - jnp.max(scores, axis=-1, keepdims=True)).astype(jnp.bfloat16)
            mixed.append(
                jnp.dot(weights, jnp.where(keep, values, one), preferred_element_type=jnp.float32)
            )
        totals = pltpu.roll(jnp.where(first, mixed[1], mixed[0]), head_dim, 1)
        return (jnp.where(first, mixed[0], mixed[1]) / totals).astype(jnp.bfloat16)

    def m_copy(k, owner):
        return pltpu.make_async_remote_copy(
            src_ref=sendbuf.at[k],
            dst_ref=mix.at[owner * groups + k],
            send_sem=m_send.at[k],
            recv_sem=m_recv.at[k],
            device_id=c_dev,
            device_id_type=MESH,
        )

    def compute(k, duties):
        for s in steps:
            finish(k, s)
        turns = 2 * blocks
        for turn in range(turns):
            b = turn % blocks
            where = slice(b * BLK, (b + 1) * BLK)
            if turn < blocks:
                sendbuf[k, where, :] = attend(k, other, b)
            else:
                mix[core * groups + k, where, :] = attend(k, core, b)
            if turn == blocks - 1:
                start(m_copy(k, core))
            for duty in duties[turn * len(duties) // turns : (turn + 1) * len(duties) // turns]:
                duty()

    spread(0)
    spread(1)
    cross(0)
    spread(2)
    cross(1)
    remote(nbuf.at[other], t_send.at[1], t_recv.at[1], c_dev).wait_recv()
    for k in range(groups):
        duties = []
        for s in steps:
            if k + 3 <= groups:
                duties.append(functools.partial(spread_one, k + 3, s))
        for s in steps:
            if k + 2 <= groups:
                duties.append(functools.partial(cross_one, k + 2, s))
        compute(k, duties)

    def o_copy(s, owner):
        where = rows_of(behind(s) * shard, shard)
        return remote(obuf.at[owner, where, :], o_send.at[s - 1], o_recv.at[s - 1], c_dev)

    for s in steps:
        finish(groups, s)
        start(o_copy(s, core))
    for k in range(groups):
        m_copy(k, other).wait_recv()

    def project(h):
        @pl.loop(0, blocks)
        def _(b):
            where = rows_of(b * BLK, BLK)
            mixed = jnp.concatenate([mix[j, where, :] for j in range(2 * groups)], axis=1)
            result = jnp.dot(mixed, obuf[h], preferred_element_type=jnp.float32)
            ids = jnp.broadcast_to(segbuf[core, 0:1, where].astype(jnp.float32), (pair, BLK)).T
            keep = jnp.concatenate([ids] * (half // pair), axis=1) >= 0.0
            out_ref[where, pl.ds(pl.multiple_of(h * half, half), half)] = jnp.where(keep, result, 0.0).astype(
                jnp.bfloat16
            )

    project(core)
    for s in steps:
        o_copy(s, other).wait_recv()
    project(other)
    for copy in pending:
        copy.wait_send()


def body(tokens, segments, qkv_weight, out_weight, shards):
    rows, width = tokens.shape
    half = width // 2
    pair = 2 * (width // HEADS)
    groups = half // pair
    blocks = rows // BLK
    vmem = pl.BlockSpec(memory_space=pltpu.VMEM)
    hbm = pl.BlockSpec(memory_space=pl.ANY)
    bf16 = jnp.bfloat16
    dma = pltpu.SemaphoreType.DMA
    sets = dma((groups + 1, shards - 1))
    return pl.pallas_call(
        functools.partial(kernel, shards),
        out_shape=jax.ShapeDtypeStruct((rows, width), bf16),
        in_specs=[vmem, vmem, hbm, hbm],
        out_specs=vmem,
        scratch_shapes=[
            pltpu.VMEM((groups, width, 3 * pair), bf16),
            pltpu.VMEM((2, width, half), bf16),
            pltpu.VMEM((2, rows, width), bf16),
            pltpu.VMEM((2, 8, rows), jnp.int32),
            pltpu.VMEM((2, blocks, BLK, BLK), jnp.float32),
            pltpu.VMEM((groups, rows, pair), bf16),
            pltpu.VMEM((2 * groups, rows, pair), bf16),
            dma((3 * groups + 2,)),
            *([sets] * 8),
            dma((shards - 1,)),
            dma((shards - 1,)),
            dma((groups,)),
            dma((groups,)),
            dma((2,)),
            dma((2,)),
        ],
        compiler_params=pltpu.CompilerParams(
            collective_id=0, has_side_effects=True, vmem_limit_bytes=63 << 20
        ),
    )(tokens, segments.reshape(1, rows), qkv_weight, out_weight)


def solution(mesh):
    return jax.shard_map(
        functools.partial(body, shards=mesh.shape["fsdp"]),
        mesh=mesh,
        in_specs=(P(("dp", "fsdp"), None), P(("dp", "fsdp")), P("fsdp", None), P("fsdp", None)),
        out_specs=P(("dp", "fsdp"), None),
        check_vma=False,
    )
```
